512 devices in a mesh: rep: 4 (over x_lo, core), fsdp: 32 (over x_hi, z), tp: 4 (over y).
Axes of the slice: x: 4 (x_hi: 2, x_lo: 2; x = x_hi * 2 + x_lo), y: 4, z: 16, core: 2. Of those that a mesh axis runs over, the one named last changes fastest.
Arguments:
- inner_weights: bfloat16 [4, 8192, 8192], P('rep', 'fsdp', 'tp'), may hold values from -6 to 6
- outer_weights: float32 [32, 128, 2, 8192], P(None, ('rep', 'fsdp'), None, 'tp'), may hold values from -6 to 6
- outer_momentum: float32 [32, 128, 2, 8192], P(None, ('rep', 'fsdp'), None, 'tp'), may hold values from -6 to 6
Outputs:
- mixed_inner: bfloat16 [4, 8192, 8192], P('rep', 'fsdp', 'tp')
- new_outer: float32 [32, 128, 2, 8192], P(None, ('rep', 'fsdp'), None, 'tp')
- new_momentum: float32 [32, 128, 2, 8192], P(None, ('rep', 'fsdp'), None, 'tp')
The draws below stay inside these ranges and needn't reach their ends.
All inputs are finite; a program needn't handle non-finite values.
Results may differ from the reference program's by a relative error of at most 0.0085.
Values may be sent and summed in bfloat16 or wider, within the bound.
No kernel may reach another device: no remote copies, remote signals or barrier semaphores. Data moves between devices by JAX's collectives and lax.ppermute only.
A program may use at most 64 MiB of HBM per device.

```python
import jax
import jax.numpy as jnp

QDIM = 8192
D = 8192
REPLICAS = 4
OWNERS = 128
GROUP = 2
N_REP = 4
N_FSDP = 32


def block_scale(rng, extent, shards, smallest, largest):
    factor_of, own = 1.0, jax.random.fold_in(rng, 6)
    for axis_at, blocks in shards:
        draws = jnp.exp(jax.random.uniform(jax.random.fold_in(own, axis_at), (blocks,), jnp.float32, smallest / len(shards), largest / len(shards)))
        factor_of = factor_of * jnp.repeat(draws, extent[axis_at] // blocks).reshape([-1 if axis == axis_at else 1 for axis in range(len(extent))])
    return factor_of


def gaussian(rng, extent, deviation, limit, shards=(), kind=jnp.bfloat16):
    values = jax.random.normal(rng, extent, jnp.float32) * deviation
    if len(shards) > 0:
        values = block_scale(rng, extent, shards, -0.22, 0.18) * values
    return jnp.clip(values, min=-limit, max=limit).astype(kind)


def setup_inputs(seed: int = 0) -> dict:
    key_list = jax.random.split(jax.random.key(seed), 4)
    inner_weights = gaussian(key_list[0], (REPLICAS, QDIM, D), 1.0, 6.0, ((0, 4), (1, 32), (2, 4)))
    outer_weights = gaussian(key_list[1], (N_FSDP, OWNERS, GROUP, D), 1.0, 6.0, ((1, 128), (3, 4)), jnp.float32)
    outer_momentum = gaussian(key_list[2], (N_FSDP, OWNERS, GROUP, D), 1.0, 6.0, ((1, 128), (3, 4)), jnp.float32)
    return dict(inner_weights=inner_weights, outer_weights=outer_weights, outer_momentum=outer_momentum)


def reference(inner_weights, outer_weights, outer_momentum):
    inner_total = jnp.zeros(outer_weights.shape, jnp.float32)
    for replica in range(N_REP):
        part = inner_weights[replica].astype(jnp.float32)
        inner_total = inner_total + part.reshape(N_FSDP, N_REP * N_FSDP, GROUP, D)
    pseudo_grad = outer_weights - inner_total / N_REP
    new_momentum = 0.9 * outer_momentum + pseudo_grad
    new_outer = outer_weights - 0.7 * (pseudo_grad + 0.9 * new_momentum)
    outer_copy = new_outer.astype(jnp.bfloat16).reshape(QDIM, D).astype(jnp.float32)
    mixed = []
    for replica in range(N_REP):
        value = 0.5 * inner_weights[replica].astype(jnp.float32) + 0.5 * outer_copy
        mixed.append(value.astype(jnp.bfloat16))
    return jnp.stack(mixed), new_outer, new_momentum
```

```python
import jax
import jax.numpy as jnp
from jax import lax
from jax.sharding import PartitionSpec as P

CORE_SWAP = [(0, 1), (1, 0), (2, 3), (3, 2)]
CHIP_SWAP = [(0, 2), (2, 0), (1, 3), (3, 1)]
F32 = jnp.float32
BF16 = jnp.bfloat16


def on_device(inner_weights, outer_weights, outer_momentum):
    shard = inner_weights[0]
    rows_here, columns = shard.shape
    replicas = lax.axis_size("rep")
    blocks = lax.axis_size("fsdp")
    group = rows_here // (replicas * blocks)
    rep = lax.axis_index("rep")
    chip, core = rep // 2, rep % 2

    parts = shard.reshape(2, 2, rows_here // 4, columns)
    mine = lax.dynamic_index_in_dim(parts, core, 1, keepdims=False)
    other = lax.dynamic_index_in_dim(parts, 1 - core, 1, keepdims=False)
    pair = mine.astype(F32) + lax.ppermute(other, "rep", CORE_SWAP).astype(F32)
    pair_mine = lax.dynamic_index_in_dim(pair, chip, 0, keepdims=False)
    pair_other = lax.dynamic_index_in_dim(pair, 1 - chip, 0, keepdims=False)
    came = lax.ppermute(pair_other.astype(BF16), "rep", CHIP_SWAP)
    total = (pair_mine + came.astype(F32)).astype(BF16)

    inner_total = lax.all_to_all(
        total.reshape(blocks, group, columns), "fsdp", split_axis=0, concat_axis=0, tiled=True
    ).astype(F32)
    outer_here = outer_weights[:, 0]
    pseudo_grad = outer_here - inner_total / replicas
    new_momentum = 0.9 * outer_momentum[:, 0] + pseudo_grad
    new_outer = outer_here - 0.7 * (pseudo_grad + 0.9 * new_momentum)
    outer_copy = new_outer.astype(BF16)

    back = lax.all_to_all(outer_copy, "fsdp", split_axis=0, concat_axis=0, tiled=True)
    back = back.reshape(rows_here // 4, columns)
    across = lax.ppermute(back, "rep", CHIP_SWAP)
    two = jnp.where(chip == 0, jnp.stack([back, across]), jnp.stack([across, back]))
    beside = lax.ppermute(two, "rep", CORE_SWAP)
    rows = jnp.where(core == 0, jnp.stack([two, beside], 1), jnp.stack([beside, two], 1))
    outer_rows = rows.reshape(rows_here, columns).astype(F32)
    mixed = (0.5 * shard.astype(F32) + 0.5 * outer_rows).astype(BF16)
    return (mixed[None], new_outer[:, None], new_momentum[:, None])


def solution(mesh):
    in_specs = (
        P("rep", "fsdp", "tp"),
        P(None, ("rep", "fsdp"), None, "tp"),
        P(None, ("rep", "fsdp"), None, "tp"),
    )
    out_specs = (
        P("rep", "fsdp", "tp"),
        P(None, ("rep", "fsdp"), None, "tp"),
        P(None, ("rep", "fsdp"), None, "tp"),
    )
    return jax.shard_map(
        on_device, mesh=mesh, in_specs=in_specs, out_specs=out_specs, check_vma=False
    )
```

```python
import jax
import jax.numpy as jnp
from jax import lax
from jax.sharding import PartitionSpec as P

CORE_SWAP = [(0, 1), (1, 0), (2, 3), (3, 2)]
CHIP_SWAP = [(0, 2), (2, 0), (1, 3), (3, 1)]
F32 = jnp.float32
BF16 = jnp.bfloat16


def on_device(inner_weights, outer_weights, outer_momentum):
    shard = inner_weights[0]
    rows_here, columns = shard.shape
    replicas = lax.axis_size("rep")
    blocks = lax.axis_size("fsdp")
    group = rows_here // (replicas * blocks)
    rep = lax.axis_index("rep")
    chip, core = rep // 2, rep % 2
    outer_here = outer_weights[:, 0]
    momentum_here = outer_momentum[:, 0]

    state_part = (-0.33 * outer_here - 0.567 * momentum_here).astype(BF16)
    state_rows = lax.all_to_all(state_part, "fsdp", split_axis=0, concat_axis=0, tiled=True)
    state_rows = state_rows.reshape(rows_here // 4, columns)

    parts = shard.reshape(2, 2, rows_here // 4, columns)
    mine = lax.dynamic_index_in_dim(parts, core, 1, keepdims=False)
    other = lax.dynamic_index_in_dim(parts, 1 - core, 1, keepdims=False)
    pair = mine.astype(F32) + lax.ppermute(other, "rep", CORE_SWAP).astype(F32)
    pair_mine = lax.dynamic_index_in_dim(pair, chip, 0, keepdims=False)
    pair_other = lax.dynamic_index_in_dim(pair, 1 - chip, 0, keepdims=False)
    came = lax.ppermute(pair_other.astype(BF16), "rep", CHIP_SWAP)
    total = pair_mine + came.astype(F32)

    inner_total = lax.all_to_all(
        total.astype(BF16).reshape(blocks, group, columns),
        "fsdp", split_axis=0, concat_axis=0, tiled=True,
    ).astype(F32)

    copy = (state_rows.astype(F32) + 0.3325 * total).astype(BF16)
    across = lax.ppermute(copy, "rep", CHIP_SWAP)
    two = jnp.where(chip == 0, jnp.stack([copy, across]), jnp.stack([across, copy]))
    beside = lax.ppermute(two, "rep", CORE_SWAP)
    rows = jnp.where(core == 0, jnp.stack([two, beside], 1), jnp.stack([beside, two], 1))
    outer_rows = rows.reshape(rows_here, columns).astype(F32)
    mixed = (0.5 * shard.astype(F32) + 0.5 * outer_rows).astype(BF16)

    pseudo_grad = outer_here - inner_total / replicas
    new_momentum = 0.9 * momentum_here + pseudo_grad
    new_outer = outer_here - 0.7 * (pseudo_grad + 0.9 * new_momentum)
    return (mixed[None], new_outer[:, None], new_momentum[:, None])


def solution(mesh):
    in_specs = (
        P("rep", "fsdp", "tp"),
        P(None, ("rep", "fsdp"), None, "tp"),
        P(None, ("rep", "fsdp"), None, "tp"),
    )
    out_specs = (
        P("rep", "fsdp", "tp"),
        P(None, ("rep", "fsdp"), None, "tp"),
        P(None, ("rep", "fsdp"), None, "tp"),
    )
    return jax.shard_map(
        on_device, mesh=mesh, in_specs=in_specs, out_specs=out_specs, check_vma=False
    )
```

```python
import jax
import jax.numpy as jnp
from jax import lax
from jax.experimental import pallas as pl
from jax.experimental.pallas import tpu as pltpu
from jax.sharding import PartitionSpec as P

F32 = jnp.float32
BF16 = jnp.bfloat16
VMEM = pl.BlockSpec(memory_space=pltpu.VMEM)
PARAMS = pltpu.CompilerParams(vmem_limit_bytes=32 * 1024 * 1024)


def cost(nbytes):
    return pl.CostEstimate(flops=0, bytes_accessed=nbytes, transcendentals=0)


def mix_kernel(rep_ref, shard_ref, *refs):
    *copy_refs, out_ref = refs
    rep = rep_ref[0]
    quarter = copy_refs[0].shape[0]
    for i, copy_ref in enumerate(copy_refs):
        rows = pl.ds(pl.multiple_of((rep ^ i) * quarter, quarter), quarter)
        value = 0.5 * shard_ref[rows, :].astype(F32) + 0.5 * copy_ref[...].astype(F32)
        out_ref[rows, :] = value.astype(BF16)


def mix(rep, shard, copies):
    return pl.pallas_call(
        mix_kernel,
        in_specs=[pl.BlockSpec(memory_space=pltpu.SMEM)] + [VMEM] * (1 + len(copies)),
        out_specs=VMEM,
        out_shape=jax.ShapeDtypeStruct(shard.shape, BF16),
        cost_estimate=cost(3 << 20),
        compiler_params=PARAMS,
    )(rep.reshape(1), shard, *copies)


def on_device(inner_weights, outer_weights, outer_momentum):
    shard = inner_weights[0]
    rows_here, columns = shard.shape
    replicas = lax.axis_size("rep")
    blocks = lax.axis_size("fsdp")
    quarter = rows_here // replicas
    group = quarter // blocks
    rep = lax.axis_index("rep")
    chip, core = rep // 2, rep % 2
    outer_here = outer_weights[:, 0]
    momentum_here = outer_momentum[:, 0]

    def exchange(value):
        return lax.all_to_all(value, "fsdp", split_axis=0, concat_axis=0, tiled=True)

    def swap(value, i):
        return lax.ppermute(value, "rep", [(r, r ^ i) for r in range(replicas)])

    state_part = (-0.33 * outer_here - 0.567 * momentum_here).astype(BF16)
    parts = shard.reshape(2, 2, quarter, columns)
    parts, state_part = lax.optimization_barrier((parts, state_part))
    state_rows = exchange(state_part).reshape(quarter, columns)

    other = lax.dynamic_index_in_dim(parts, 1 - core, 1, keepdims=False)
    mine = lax.dynamic_index_in_dim(parts, core, 1, keepdims=False)
    pair = mine.astype(F32) + swap(other, 1).astype(F32)
    pair_mine = lax.dynamic_index_in_dim(pair, chip, 0, keepdims=False)
    pair_other = lax.dynamic_index_in_dim(pair, 1 - chip, 0, keepdims=False)
    total = pair_mine + swap(pair_other.astype(BF16), 2).astype(F32)

    sent = total.astype(BF16).reshape(blocks, group, columns)
    sent, total = lax.optimization_barrier((sent, total))
    inner_total = exchange(sent)

    copy = (state_rows.astype(F32) + 0.3325 * total).astype(BF16)
    beside = swap(copy, 1)
    across = swap(copy, 2)
    diagonal = swap(across, 1)
    pseudo_grad = outer_here - inner_total.astype(F32) / replicas
    new_momentum = 0.9 * momentum_here + pseudo_grad
    new_outer = outer_here - 0.7 * (pseudo_grad + 0.9 * new_momentum)
    mixed = mix(rep, shard, [copy, beside, across, diagonal])
    return (mixed[None], new_outer[:, None], new_momentum[:, None])


def solution(mesh):
    in_specs = (
        P("rep", "fsdp", "tp"),
        P(None, ("rep", "fsdp"), None, "tp"),
        P(None, ("rep", "fsdp"), None, "tp"),
    )
    out_specs = (
        P("rep", "fsdp", "tp"),
        P(None, ("rep", "fsdp"), None, "tp"),
        P(None, ("rep", "fsdp"), None, "tp"),
    )
    return jax.shard_map(
        on_device, mesh=mesh, in_specs=in_specs, out_specs=out_specs, check_vma=False
    )
```

```python
import jax
import jax.numpy as jnp
from jax import lax
from jax.experimental import pallas as pl
from jax.experimental.pallas import tpu as pltpu
from jax.sharding import PartitionSpec as P

F32 = jnp.float32
BF16 = jnp.bfloat16
VMEM = pl.BlockSpec(memory_space=pltpu.VMEM)
SMEM = pl.BlockSpec(memory_space=pltpu.SMEM)
ANY = pl.BlockSpec(memory_space=pl.ANY)
PARAMS = pltpu.CompilerParams(vmem_limit_bytes=32 * 1024 * 1024)
FIRST = 11


def cost(nbytes):
    return pl.CostEstimate(flops=0, bytes_accessed=nbytes, transcendentals=0)


def segments(blocks):
    ring = blocks // 2
    late = ring - FIRST
    for half in (0, ring):
        yield half, half + FIRST, late
        yield half + late, half, FIRST


def first_kernel(chip_ref, weights_ref, momentum_ref, parts_ref, state_ref, other_ref, *scratch):
    weights, momentum, state, sems = scratch
    other = pltpu.make_async_copy(parts_ref.at[1 - chip_ref[0]], other_ref, sems.at[3, 0])
    runs = list(segments(weights.shape[0]))
    loads, stores = [], []
    for n, (place, index, length) in enumerate(runs):
        rows = pl.ds(index, length)
        for m, (source, target) in enumerate(((weights_ref, weights), (momentum_ref, momentum))):
            copy = pltpu.make_async_copy(source.at[rows], target.at[rows], sems.at[m, n])
            copy.start()
            loads.append(copy)
        if n == 0:
            other.start()
    for n, (place, index, length) in enumerate(runs):
        loads[2 * n].wait()
        loads[2 * n + 1].wait()
        rows, places = pl.ds(index, length), pl.ds(place, length)
        state[places] = (-0.33 * weights[rows] - 0.567 * momentum[rows]).astype(BF16)
        copy = pltpu.make_async_copy(state.at[places], state_ref.at[places], sems.at[2, n])
        copy.start()
        stores.append(copy)
    other.wait()
    for copy in stores:
        copy.wait()


def state_and_other(chip, weights, momentum, parts):
    shape = weights.shape
    return pl.pallas_call(
        first_kernel,
        in_specs=[SMEM, ANY, ANY, ANY],
        out_specs=[ANY, VMEM],
        out_shape=[
            jax.ShapeDtypeStruct(shape, BF16),
            jax.ShapeDtypeStruct(parts.shape[1:], BF16),
        ],
        scratch_shapes=[
            pltpu.VMEM(shape, F32),
            pltpu.VMEM(shape, F32),
            pltpu.VMEM(shape, BF16),
            pltpu.SemaphoreType.DMA((4, 4)),
        ],
        cost_estimate=cost(3 << 20),
    )(chip.reshape(1), weights, momentum, parts)


def update_kernel(total_ref, weights_ref, momentum_ref, outer_ref, out_momentum_ref):
    for place, index, length in segments(weights_ref.shape[0]):
        rows = pl.ds(index, length)
        weights = weights_ref[rows]
        pseudo_grad = weights - 0.25 * total_ref[pl.ds(place, length)].astype(F32)
        momentum = 0.9 * momentum_ref[rows] + pseudo_grad
        out_momentum_ref[rows] = momentum
        outer_ref[rows] = weights - 0.7 * (pseudo_grad + 0.9 * momentum)


def update(total, weights, momentum):
    return pl.pallas_call(
        update_kernel,
        in_specs=[VMEM] * 3,
        out_specs=[VMEM] * 2,
        out_shape=[jax.ShapeDtypeStruct(weights.shape, F32)] * 2,
        cost_estimate=cost(3 << 20),
        compiler_params=PARAMS,
    )(total, weights, momentum)


def mix_kernel(rep_ref, shard_ref, *refs):
    *copy_refs, out_ref = refs
    rep = rep_ref[0]
    quarter = copy_refs[0].shape[0]
    for i, copy_ref in enumerate(copy_refs):
        rows = pl.ds(pl.multiple_of((rep ^ i) * quarter, quarter), quarter)
        value = 0.5 * shard_ref[rows, :].astype(F32) + 0.5 * copy_ref[...].astype(F32)
        out_ref[rows, :] = value.astype(BF16)


def mix(rep, shard, copies):
    return pl.pallas_call(
        mix_kernel,
        in_specs=[SMEM] + [VMEM] * (1 + len(copies)),
        out_specs=VMEM,
        out_shape=jax.ShapeDtypeStruct(shard.shape, BF16),
        cost_estimate=cost(3 << 20),
        compiler_params=PARAMS,
    )(rep.reshape(1), shard, *copies)


def on_device(inner_weights, outer_weights, outer_momentum):
    shard = inner_weights[0]
    rows_here, columns = shard.shape
    replicas = lax.axis_size("rep")
    blocks = lax.axis_size("fsdp")
    quarter = rows_here // replicas
    group = quarter // blocks
    rep = lax.axis_index("rep")
    chip, core = rep // 2, rep % 2
    outer_here = outer_weights[:, 0]
    momentum_here = outer_momentum[:, 0]
    ring = blocks // 2
    order = [half + (FIRST + z) % ring for half in (0, ring) for z in range(ring)]

    def exchange(value):
        return lax.all_to_all(
            value, "fsdp", split_axis=0, concat_axis=0, axis_index_groups=[order], tiled=True
        )

    def turn(value, by):
        halves = value.reshape(2, ring, *value.shape[1:])
        halves = jnp.concatenate([halves[:, by:], halves[:, :by]], axis=1)
        return halves.reshape(value.shape)

    def swap(value, i):
        return lax.ppermute(value, "rep", [(r, r ^ i) for r in range(replicas)])

    parts = shard.reshape(2, 2 * quarter, columns)
    state_part, other = state_and_other(chip, outer_here, momentum_here, parts)
    state_rows = turn(exchange(state_part), ring - FIRST).reshape(quarter, columns)

    mine = lax.dynamic_index_in_dim(parts, chip, 0, keepdims=False)
    pair = (mine.astype(F32) + swap(other, 2).astype(F32)).reshape(2, quarter, columns)
    pair_mine = lax.dynamic_index_in_dim(pair, core, 0, keepdims=False)
    pair_other = lax.dynamic_index_in_dim(pair, 1 - core, 0, keepdims=False)
    total = pair_mine + swap(pair_other.astype(BF16), 1).astype(F32)

    sent = turn(total.astype(BF16).reshape(blocks, group, columns), FIRST)
    sent, total = lax.optimization_barrier((sent, total))
    inner_total = exchange(sent)

    copy = (state_rows.astype(F32) + 0.3325 * total).astype(BF16)
    beside = swap(copy, 1)
    across = swap(copy, 2)
    diagonal = swap(across, 1)
    mixed = mix(rep, shard, [copy, beside, across, diagonal])

    new_outer, new_momentum = update(inner_total, outer_here, momentum_here)
    return (mixed[None], new_outer[:, None], new_momentum[:, None])


def solution(mesh):
    in_specs = (
        P("rep", "fsdp", "tp"),
        P(None, ("rep", "fsdp"), None, "tp"),
        P(None, ("rep", "fsdp"), None, "tp"),
    )
    out_specs = (
        P("rep", "fsdp", "tp"),
        P(None, ("rep", "fsdp"), None, "tp"),
        P(None, ("rep", "fsdp"), None, "tp"),
    )
    return jax.shard_map(
        on_device, mesh=mesh, in_specs=in_specs, out_specs=out_specs, check_vma=False
    )
```

```python
import jax
import jax.numpy as jnp
from jax import lax
from jax.experimental import pallas as pl
from jax.experimental.pallas import tpu as pltpu
from jax.sharding import PartitionSpec as P

F32 = jnp.float32
BF16 = jnp.bfloat16
VMEM = pl.BlockSpec(memory_space=pltpu.VMEM)
SMEM = pl.BlockSpec(memory_space=pltpu.SMEM)
HBM = pl.BlockSpec(memory_space=pltpu.HBM)
PARAMS = pltpu.CompilerParams(vmem_limit_bytes=16 * 1024 * 1024)
FIRST = 11


def cost(nbytes):
    return pl.CostEstimate(flops=0, bytes_accessed=nbytes, transcendentals=0)


def segments(blocks):
    ring = blocks // 2
    late = ring - FIRST
    for half in (0, ring):
        yield half, half + FIRST, late
        yield half + late, half, FIRST


def first_kernel(chip_ref, weights_ref, momentum_ref, parts_ref, state_ref, other_ref, *scratch):
    weights, momentum, state, other, sems = scratch
    runs = sorted(segments(weights.shape[0]), key=lambda run: -run[2])
    take = pltpu.make_async_copy(parts_ref.at[1 - chip_ref[0]], other, sems.at[3, 0])
    give = pltpu.make_async_copy(other, other_ref, sems.at[3, 1])
    take.start()
    loads, stores = [], [give]
    for n, (place, index, length) in enumerate(runs):
        rows = pl.ds(index, length)
        for m, (source, target) in enumerate(((weights_ref, weights), (momentum_ref, momentum))):
            copy = pltpu.make_async_copy(source.at[rows], target.at[rows], sems.at[m, n])
            copy.start()
            loads.append(copy)
    take.wait()
    give.start()
    for n, (place, index, length) in enumerate(runs):
        loads[2 * n].wait()
        loads[2 * n + 1].wait()
        rows, places = pl.ds(index, length), pl.ds(place, length)
        state[places] = (-0.33 * weights[rows] - 0.567 * momentum[rows]).astype(BF16)
        copy = pltpu.make_async_copy(state.at[places], state_ref.at[places], sems.at[2, n])
        copy.start()
        stores.append(copy)
    for copy in stores:
        copy.wait()


def state_and_other(chip, weights, momentum, parts):
    shape = weights.shape
    return pl.pallas_call(
        first_kernel,
        in_specs=[SMEM, HBM, HBM, HBM],
        out_specs=[HBM, HBM],
        out_shape=[
            jax.ShapeDtypeStruct(shape, BF16),
            jax.ShapeDtypeStruct(parts.shape[1:], BF16),
        ],
        scratch_shapes=[
            pltpu.VMEM(shape, F32),
            pltpu.VMEM(shape, F32),
            pltpu.VMEM(shape, BF16),
            pltpu.VMEM(parts.shape[1:], BF16),
            pltpu.SemaphoreType.DMA((4, 4)),
        ],
        cost_estimate=cost(3 << 20),
    )(chip.reshape(1), weights, momentum, parts)


def update_kernel(total_ref, weights_ref, momentum_ref, outer_ref, out_momentum_ref, outer, out_momentum, sems):
    stores = []
    for n, (place, index, length) in enumerate(segments(weights_ref.shape[0])):
        rows = pl.ds(index, length)
        weights = weights_ref[rows]
        pseudo_grad = weights - 0.25 * total_ref[pl.ds(place, length)].astype(F32)
        momentum = 0.9 * momentum_ref[rows] + pseudo_grad
        out_momentum[rows] = momentum
        outer[rows] = weights - 0.7 * (pseudo_grad + 0.9 * momentum)
        for m, (value, ref) in enumerate(((outer, outer_ref), (out_momentum, out_momentum_ref))):
            copy = pltpu.make_async_copy(value.at[rows], ref.at[rows], sems.at[m, n])
            copy.start()
            stores.append(copy)
    for copy in stores:
        copy.wait()


def update(total, weights, momentum):
    return pl.pallas_call(
        update_kernel,
        in_specs=[VMEM] * 3,
        out_specs=[HBM] * 2,
        out_shape=[jax.ShapeDtypeStruct(weights.shape, F32)] * 2,
        scratch_shapes=[
            pltpu.VMEM(weights.shape, F32),
            pltpu.VMEM(weights.shape, F32),
            pltpu.SemaphoreType.DMA((2, 4)),
        ],
        cost_estimate=cost(3 << 20),
        compiler_params=PARAMS,
    )(total, weights, momentum)


def mixed_rows(shard, copy):
    return (0.5 * shard.astype(F32) + 0.5 * copy.astype(F32)).astype(BF16)


def rows_of(place, quarter):
    return pl.ds(pl.multiple_of(place * quarter, quarter), quarter)


def mix_kernel(rep_ref, shard_ref, *refs):
    *copy_refs, out_ref, rest_ref, shard, out, sems = refs
    rep = rep_ref[0]
    quarter = rest_ref.shape[0]
    last = len(copy_refs)
    rows = [rows_of(rep ^ i, quarter) for i in range(last + 1)]
    loads = [
        pltpu.make_async_copy(shard_ref.at[rows[i]], shard.at[i], sems.at[0, i])
        for i in range(last)
    ]
    loads.append(pltpu.make_async_copy(shard_ref.at[rows[last]], rest_ref, sems.at[0, last]))
    stores = [
        pltpu.make_async_copy(out.at[i], out_ref.at[rows[i]], sems.at[1, i]) for i in range(last)
    ]
    for load in loads:
        load.start()
    for i, copy_ref in enumerate(copy_refs):
        loads[i].wait()
        out[i] = mixed_rows(shard[i], copy_ref[...])
        stores[i].start()
    loads[last].wait()
    for store in stores:
        store.wait()


def mix(rep, shard, copies):
    quarter = copies[0].shape
    count = len(copies)
    return pl.pallas_call(
        mix_kernel,
        in_specs=[SMEM, HBM] + [VMEM] * count,
        out_specs=[HBM, VMEM],
        out_shape=[
            jax.ShapeDtypeStruct(shard.shape, BF16),
            jax.ShapeDtypeStruct(quarter, BF16),
        ],
        scratch_shapes=[
            pltpu.VMEM((count, *quarter), BF16),
            pltpu.VMEM((count, *quarter), BF16),
            pltpu.SemaphoreType.DMA((2, count + 1)),
        ],
        cost_estimate=cost(3 << 19),
        compiler_params=PARAMS,
    )(rep.reshape(1), shard, *copies)


def rest_kernel(place_ref, shard_ref, copy_ref, before_ref, out_ref, out, sem):
    del before_ref
    out[...] = mixed_rows(shard_ref[...], copy_ref[...])
    rows = rows_of(place_ref[0], out.shape[0])
    store = pltpu.make_async_copy(out, out_ref.at[rows], sem)
    store.start()
    store.wait()


def mix_rest(place, shard, copy, before):
    return pl.pallas_call(
        rest_kernel,
        in_specs=[SMEM, VMEM, VMEM, HBM],
        out_specs=HBM,
        out_shape=jax.ShapeDtypeStruct(before.shape, BF16),
        scratch_shapes=[pltpu.VMEM(copy.shape, BF16), pltpu.SemaphoreType.DMA],
        input_output_aliases={3: 0},
        cost_estimate=cost(3 << 18),
        compiler_params=PARAMS,
    )(place.reshape(1), shard, copy, before)


def on_device(inner_weights, outer_weights, outer_momentum):
    shard = inner_weights[0]
    rows_here, columns = shard.shape
    replicas = lax.axis_size("rep")
    blocks = lax.axis_size("fsdp")
    quarter = rows_here // replicas
    group = quarter // blocks
    rep = lax.axis_index("rep")
    chip, core = rep // 2, rep % 2
    outer_here = outer_weights[:, 0]
    momentum_here = outer_momentum[:, 0]
    ring = blocks // 2
    order = [half + (FIRST + z) % ring for half in (0, ring) for z in range(ring)]

    def exchange(value):
        return lax.all_to_all(
            value, "fsdp", split_axis=0, concat_axis=0, axis_index_groups=[order], tiled=True
        )

    def turn(value, by):
        halves = value.reshape(2, ring, *value.shape[1:])
        halves = jnp.concatenate([halves[:, by:], halves[:, :by]], axis=1)
        return halves.reshape(value.shape)

    def swap(value, i):
        return lax.ppermute(value, "rep", [(r, r ^ i) for r in range(replicas)])

    parts = shard.reshape(2, 2 * quarter, columns)
    state_part, other = state_and_other(chip, outer_here, momentum_here, parts)
    state_rows = turn(exchange(state_part), ring - FIRST).reshape(quarter, columns)

    mine = lax.dynamic_index_in_dim(parts, chip, 0, keepdims=False)
    pair = (mine.astype(F32) + swap(other, 2).astype(F32)).reshape(2, quarter, columns)
    pair_mine = lax.dynamic_index_in_dim(pair, core, 0, keepdims=False)
    pair_other = lax.dynamic_index_in_dim(pair, 1 - core, 0, keepdims=False)
    total = pair_mine + swap(pair_other.astype(BF16), 1).astype(F32)

    sent = turn(total.astype(BF16).reshape(blocks, group, columns), FIRST)
    sent, total = lax.optimization_barrier((sent, total))
    inner_total = exchange(sent)

    copy = (state_rows.astype(F32) + 0.3325 * total).astype(BF16)
    beside = swap(copy, 1)
    across = swap(copy, 2)
    diagonal = swap(across, 1)
    mixed, rest = mix(rep, shard, [copy, beside, across])
    mixed = mix_rest(rep ^ 3, rest, diagonal, mixed)

    new_outer, new_momentum = update(inner_total, outer_here, momentum_here)
    return (mixed[None], new_outer[:, None], new_momentum[:, None])


def solution(mesh):
    in_specs = (
        P("rep", "fsdp", "tp"),
        P(None, ("rep", "fsdp"), None, "tp"),
        P(None, ("rep", "fsdp"), None, "tp"),
    )
    out_specs = (
        P("rep", "fsdp", "tp"),
        P(None, ("rep", "fsdp"), None, "tp"),
        P(None, ("rep", "fsdp"), None, "tp"),
    )
    return jax.shard_map(
        on_device, mesh=mesh, in_specs=in_specs, out_specs=out_specs, check_vma=False
    )
```

```python
import jax
import jax.numpy as jnp
from jax import lax
from jax.experimental import pallas as pl
from jax.experimental.pallas import tpu as pltpu
from jax.sharding import PartitionSpec as P

F32 = jnp.float32
BF16 = jnp.bfloat16
VMEM = pl.BlockSpec(memory_space=pltpu.VMEM)
SMEM = pl.BlockSpec(memory_space=pltpu.SMEM)
HBM = pl.BlockSpec(memory_space=pltpu.HBM)
PARAMS = pltpu.CompilerParams(vmem_limit_bytes=8 * 1024 * 1024)
FIRST = 11


def cost(nbytes):
    return pl.CostEstimate(flops=0, bytes_accessed=nbytes, transcendentals=0)


def segments(blocks):
    ring = blocks // 2
    late = ring - FIRST
    for half in (0, ring):
        yield half, half + FIRST, late
        yield half + late, half, FIRST


def first_kernel(chip_ref, weights_ref, momentum_ref, parts_ref, state_ref, other_ref, *scratch):
    weights, momentum, state, other, sems = scratch
    runs = []
    for place, index, length in segments(weights.shape[0]):
        half = length // 2
        runs += [(place, index, half), (place + half, index + half, length - half)]
    runs.sort(key=lambda run: -run[2])
    takes, gives = [], []
    quarter = other.shape[0] // 4
    for n in range(4):
        rows = pl.ds(n * quarter, quarter)
        source = parts_ref.at[1 - chip_ref[0], rows]
        takes.append(pltpu.make_async_copy(source, other.at[rows], sems.at[3, n]))
        gives.append(pltpu.make_async_copy(other.at[rows], other_ref.at[rows], sems.at[3, 4 + n]))
        takes[n].start()
    loads, stores = [], []
    for n, (place, index, length) in enumerate(runs):
        rows = pl.ds(index, length)
        for m, (source, target) in enumerate(((weights_ref, weights), (momentum_ref, momentum))):
            copy = pltpu.make_async_copy(source.at[rows], target.at[rows], sems.at[m, n])
            copy.start()
            loads.append(copy)
    for take, give in zip(takes, gives):
        take.wait()
        give.start()
    for n, (place, index, length) in enumerate(runs):
        loads[2 * n].wait()
        loads[2 * n + 1].wait()
        rows, places = pl.ds(index, length), pl.ds(place, length)
        state[places] = (-0.33 * weights[rows] - 0.567 * momentum[rows]).astype(BF16)
        copy = pltpu.make_async_copy(state.at[places], state_ref.at[places], sems.at[2, n])
        copy.start()
        stores.append(copy)
    for copy in gives + stores:
        copy.wait()


def state_and_other(chip, weights, momentum, parts):
    shape = weights.shape
    return pl.pallas_call(
        first_kernel,
        in_specs=[SMEM, HBM, HBM, HBM],
        out_specs=[HBM, HBM],
        out_shape=[
            jax.ShapeDtypeStruct(shape, BF16),
            jax.ShapeDtypeStruct(parts.shape[1:], BF16),
        ],
        scratch_shapes=[
            pltpu.VMEM(shape, F32),
            pltpu.VMEM(shape, F32),
            pltpu.VMEM(shape, BF16),
            pltpu.VMEM(parts.shape[1:], BF16),
            pltpu.SemaphoreType.DMA((4, 8)),
        ],
        cost_estimate=cost(3 << 20),
    )(chip.reshape(1), weights, momentum, parts)


def update_kernel(total_ref, weights_ref, momentum_ref, outer_ref, out_momentum_ref, outer, out_momentum, sems):
    stores = []
    for n, (place, index, length) in enumerate(segments(weights_ref.shape[0])):
        rows = pl.ds(index, length)
        weights = weights_ref[rows]
        pseudo_grad = weights - 0.25 * total_ref[pl.ds(place, length)].astype(F32)
        momentum = 0.9 * momentum_ref[rows] + pseudo_grad
        out_momentum[rows] = momentum
        outer[rows] = weights - 0.7 * (pseudo_grad + 0.9 * momentum)
        for m, (value, ref) in enumerate(((outer, outer_ref), (out_momentum, out_momentum_ref))):
            copy = pltpu.make_async_copy(value.at[rows], ref.at[rows], sems.at[m, n])
            copy.start()
            stores.append(copy)
    for copy in stores:
        copy.wait()


def update(total, weights, momentum):
    return pl.pallas_call(
        update_kernel,
        in_specs=[VMEM] * 3,
        out_specs=[HBM] * 2,
        out_shape=[jax.ShapeDtypeStruct(weights.shape, F32)] * 2,
        scratch_shapes=[
            pltpu.VMEM(weights.shape, F32),
            pltpu.VMEM(weights.shape, F32),
            pltpu.SemaphoreType.DMA((2, 4)),
        ],
        cost_estimate=cost(3 << 20),
        compiler_params=PARAMS,
    )(total, weights, momentum)


def mixed_rows(shard, copy):
    return (0.5 * shard.astype(F32) + 0.5 * copy.astype(F32)).astype(BF16)


def rows_of(place, quarter):
    return pl.ds(pl.multiple_of(place * quarter, quarter), quarter)


def mix_kernel(rep_ref, shard_ref, *refs):
    *copy_refs, out_ref, rest_ref, shard, out, sems = refs
    rep = rep_ref[0]
    quarter = rest_ref.shape[0]
    last = len(copy_refs)
    rows = [rows_of(rep ^ i, quarter) for i in range(last + 1)]
    loads = [
        pltpu.make_async_copy(shard_ref.at[rows[i]], shard.at[i], sems.at[0, i])
        for i in range(last)
    ]
    loads.append(pltpu.make_async_copy(shard_ref.at[rows[last]], rest_ref, sems.at[0, last]))
    stores = [
        pltpu.make_async_copy(out.at[i], out_ref.at[rows[i]], sems.at[1, i]) for i in range(last)
    ]
    for load in loads:
        load.start()
    for i, copy_ref in enumerate(copy_refs):
        loads[i].wait()
        out[i] = mixed_rows(shard[i], copy_ref[...])
        stores[i].start()
    loads[last].wait()
    for store in stores:
        store.wait()


def mix(rep, shard, copies):
    quarter = copies[0].shape
    count = len(copies)
    return pl.pallas_call(
        mix_kernel,
        in_specs=[SMEM, HBM] + [VMEM] * count,
        out_specs=[HBM, VMEM],
        out_shape=[
            jax.ShapeDtypeStruct(shard.shape, BF16),
            jax.ShapeDtypeStruct(quarter, BF16),
        ],
        scratch_shapes=[
            pltpu.VMEM((count, *quarter), BF16),
            pltpu.VMEM((count, *quarter), BF16),
            pltpu.SemaphoreType.DMA((2, count + 1)),
        ],
        cost_estimate=cost(1 << 17),
        compiler_params=PARAMS,
    )(rep.reshape(1), shard, *copies)


def rest_kernel(place_ref, shard_ref, copy_ref, before_ref, out_ref, out, sem):
    del before_ref
    out[...] = mixed_rows(shard_ref[...], copy_ref[...])
    rows = rows_of(place_ref[0], out.shape[0])
    store = pltpu.make_async_copy(out, out_ref.at[rows], sem)
    store.start()
    store.wait()


def mix_rest(place, shard, copy, before):
    return pl.pallas_call(
        rest_kernel,
        in_specs=[SMEM, VMEM, VMEM, HBM],
        out_specs=HBM,
        out_shape=jax.ShapeDtypeStruct(before.shape, BF16),
        scratch_shapes=[pltpu.VMEM(copy.shape, BF16), pltpu.SemaphoreType.DMA],
        input_output_aliases={3: 0},
        cost_estimate=cost(1 << 16),
        compiler_params=PARAMS,
    )(place.reshape(1), shard, copy, before)


def on_device(inner_weights, outer_weights, outer_momentum):
    shard = inner_weights[0]
    rows_here, columns = shard.shape
    replicas = lax.axis_size("rep")
    blocks = lax.axis_size("fsdp")
    quarter = rows_here // replicas
    group = quarter // blocks
    rep = lax.axis_index("rep")
    chip, core = rep // 2, rep % 2
    outer_here = outer_weights[:, 0]
    momentum_here = outer_momentum[:, 0]
    ring = blocks // 2
    order = [half + (FIRST + z) % ring for half in (0, ring) for z in range(ring)]

    def exchange(value):
        return lax.all_to_all(
            value, "fsdp", split_axis=0, concat_axis=0, axis_index_groups=[order], tiled=True
        )

    def turn(value, by):
        halves = value.reshape(2, ring, *value.shape[1:])
        halves = jnp.concatenate([halves[:, by:], halves[:, :by]], axis=1)
        return halves.reshape(value.shape)

    def swap(value, i):
        return lax.ppermute(value, "rep", [(r, r ^ i) for r in range(replicas)])

    parts = shard.reshape(2, 2 * quarter, columns)
    state_part, other = state_and_other(chip, outer_here, momentum_here, parts)
    state_rows = turn(exchange(state_part), ring - FIRST).reshape(quarter, columns)

    mine = lax.dynamic_index_in_dim(parts, chip, 0, keepdims=False)
    pair = (mine.astype(F32) + swap(other, 2).astype(F32)).reshape(2, quarter, columns)
    pair_mine = lax.dynamic_index_in_dim(pair, core, 0, keepdims=False)
    pair_other = lax.dynamic_index_in_dim(pair, 1 - core, 0, keepdims=False)
    total = pair_mine + swap(pair_other.astype(BF16), 1).astype(F32)

    sent = turn(total.astype(BF16).reshape(blocks, group, columns), FIRST)
    sent, total = lax.optimization_barrier((sent, total))
    inner_total = exchange(sent)

    copy = (state_rows.astype(F32) + 0.3325 * total).astype(BF16)
    beside = swap(copy, 1)
    across = swap(copy, 2)
    diagonal = swap(across, 1)
    mixed, rest = mix(rep, shard, [copy, beside, across])
    mixed = mix_rest(rep ^ 3, rest, diagonal, mixed)

    new_outer, new_momentum = update(inner_total, outer_here, momentum_here)
    return (mixed[None], new_outer[:, None], new_momentum[:, None])


def solution(mesh):
    in_specs = (
        P("rep", "fsdp", "tp"),
        P(None, ("rep", "fsdp"), None, "tp"),
        P(None, ("rep", "fsdp"), None, "tp"),
    )
    out_specs = (
        P("rep", "fsdp", "tp"),
        P(None, ("rep", "fsdp"), None, "tp"),
        P(None, ("rep", "fsdp"), None, "tp"),
    )
    return jax.shard_map(
        on_device, mesh=mesh, in_specs=in_specs, out_specs=out_specs, check_vma=False
    )
```

```python
import jax
import jax.numpy as jnp
from jax import lax
from jax.experimental import pallas as pl
from jax.experimental.pallas import tpu as pltpu
from jax.sharding import PartitionSpec as P

F32 = jnp.float32
BF16 = jnp.bfloat16
VMEM = pl.BlockSpec(memory_space=pltpu.VMEM)
SMEM = pl.BlockSpec(memory_space=pltpu.SMEM)
HBM = pl.BlockSpec(memory_space=pltpu.HBM)
PARAMS = pltpu.CompilerParams(vmem_limit_bytes=8 * 1024 * 1024)
FIRST = 11


def cost(nbytes):
    return pl.CostEstimate(flops=0, bytes_accessed=nbytes, transcendentals=0)


def segments(blocks):
    ring = blocks // 2
    late = ring - FIRST
    for half in (0, ring):
        yield half, half + FIRST, late
        yield half + late, half, FIRST


def first_kernel(chip_ref, weights_ref, momentum_ref, parts_ref, state_ref, other_ref, *scratch):
    weights, momentum, state, other, sems = scratch
    runs = []
    for place, index, length in segments(weights.shape[0]):
        half = length // 2
        runs += [(place, index, half), (place + half, index + half, length - half)]
    runs.sort(key=lambda run: -run[2])
    takes, gives = [], []
    quarter = other.shape[0] // 4
    for n in range(4):
        rows = pl.ds(n * quarter, quarter)
        source = parts_ref.at[1 - chip_ref[0], rows]
        takes.append(pltpu.make_async_copy(source, other.at[rows], sems.at[3, n]))
        gives.append(pltpu.make_async_copy(other.at[rows], other_ref.at[rows], sems.at[3, 4 + n]))
        takes[n].start()
    loads, stores = [], []
    for n, (place, index, length) in enumerate(runs):
        rows = pl.ds(index, length)
        for m, (source, target) in enumerate(((weights_ref, weights), (momentum_ref, momentum))):
            copy = pltpu.make_async_copy(source.at[rows], target.at[rows], sems.at[m, n])
            copy.start()
            loads.append(copy)
    for take, give in zip(takes, gives):
        take.wait()
        give.start()
    for n, (place, index, length) in enumerate(runs):
        loads[2 * n].wait()
        loads[2 * n + 1].wait()
        rows, places = pl.ds(index, length), pl.ds(place, length)
        state[places] = (-0.33 * weights[rows] - 0.567 * momentum[rows]).astype(BF16)
        copy = pltpu.make_async_copy(state.at[places], state_ref.at[places], sems.at[2, n])
        copy.start()
        stores.append(copy)
    for copy in gives + stores:
        copy.wait()


def state_and_other(chip, weights, momentum, parts):
    shape = weights.shape
    return pl.pallas_call(
        first_kernel,
        in_specs=[SMEM, HBM, HBM, HBM],
        out_specs=[HBM, HBM],
        out_shape=[
            jax.ShapeDtypeStruct(shape, BF16),
            jax.ShapeDtypeStruct(parts.shape[1:], BF16),
        ],
        scratch_shapes=[
            pltpu.VMEM(shape, F32),
            pltpu.VMEM(shape, F32),
            pltpu.VMEM(shape, BF16),
            pltpu.VMEM(parts.shape[1:], BF16),
            pltpu.SemaphoreType.DMA((4, 8)),
        ],
        cost_estimate=cost(3 << 20),
    )(chip.reshape(1), weights, momentum, parts)


def update_kernel(total_ref, weights_ref, momentum_ref, outer_ref, out_momentum_ref, outer, out_momentum, sems):
    stores = []
    runs = sorted(segments(weights_ref.shape[0]), key=lambda run: -run[2])
    for n, (place, index, length) in enumerate(runs):
        rows = pl.ds(index, length)
        weights = weights_ref[rows]
        pseudo_grad = weights - 0.25 * total_ref[pl.ds(place, length)].astype(F32)
        momentum = 0.9 * momentum_ref[rows] + pseudo_grad
        out_momentum[rows] = momentum
        outer[rows] = weights - 0.7 * (pseudo_grad + 0.9 * momentum)
        for m, (value, ref) in enumerate(((outer, outer_ref), (out_momentum, out_momentum_ref))):
            copy = pltpu.make_async_copy(value.at[rows], ref.at[rows], sems.at[m, n])
            copy.start()
            stores.append(copy)
    for copy in stores:
        copy.wait()


def update(total, weights, momentum):
    return pl.pallas_call(
        update_kernel,
        in_specs=[VMEM] * 3,
        out_specs=[HBM] * 2,
        out_shape=[jax.ShapeDtypeStruct(weights.shape, F32)] * 2,
        scratch_shapes=[
            pltpu.VMEM(weights.shape, F32),
            pltpu.VMEM(weights.shape, F32),
            pltpu.SemaphoreType.DMA((2, 4)),
        ],
        cost_estimate=cost(3 << 20),
        compiler_params=PARAMS,
    )(total, weights, momentum)


def mixed_rows(shard, copy):
    return (0.5 * shard.astype(F32) + 0.5 * copy.astype(F32)).astype(BF16)


def rows_of(place, quarter):
    return pl.ds(pl.multiple_of(place * quarter, quarter), quarter)


def mix_kernel(rep_ref, shard_ref, *refs):
    *copy_refs, out_ref, rest_ref, shard, out, sems = refs
    rep = rep_ref[0]
    quarter = rest_ref.shape[0]
    last = len(copy_refs)
    rows = [rows_of(rep ^ i, quarter) for i in range(last + 1)]
    loads = [
        pltpu.make_async_copy(shard_ref.at[rows[i]], shard.at[i], sems.at[0, i])
        for i in range(last)
    ]
    loads.append(pltpu.make_async_copy(shard_ref.at[rows[last]], rest_ref, sems.at[0, last]))
    stores = [
        pltpu.make_async_copy(out.at[i], out_ref.at[rows[i]], sems.at[1, i]) for i in range(last)
    ]
    for load in loads:
        load.start()
    for i, copy_ref in enumerate(copy_refs):
        loads[i].wait()
        out[i] = mixed_rows(shard[i], copy_ref[...])
        stores[i].start()
    loads[last].wait()
    for store in stores:
        store.wait()


def mix(rep, shard, copies):
    quarter = copies[0].shape
    count = len(copies)
    return pl.pallas_call(
        mix_kernel,
        in_specs=[SMEM, HBM] + [VMEM] * count,
        out_specs=[HBM, VMEM],
        out_shape=[
            jax.ShapeDtypeStruct(shard.shape, BF16),
            jax.ShapeDtypeStruct(quarter, BF16),
        ],
        scratch_shapes=[
            pltpu.VMEM((count, *quarter), BF16),
            pltpu.VMEM((count, *quarter), BF16),
            pltpu.SemaphoreType.DMA((2, count + 1)),
        ],
        cost_estimate=cost(1 << 17),
        compiler_params=PARAMS,
    )(rep.reshape(1), shard, *copies)


def rest_kernel(place_ref, shard_ref, copy_ref, before_ref, out_ref, out, sem):
    del before_ref
    out[...] = mixed_rows(shard_ref[...], copy_ref[...])
    rows = rows_of(place_ref[0], out.shape[0])
    store = pltpu.make_async_copy(out, out_ref.at[rows], sem)
    store.start()
    store.wait()


def mix_rest(place, shard, copy, before):
    return pl.pallas_call(
        rest_kernel,
        in_specs=[SMEM, VMEM, VMEM, HBM],
        out_specs=HBM,
        out_shape=jax.ShapeDtypeStruct(before.shape, BF16),
        scratch_shapes=[pltpu.VMEM(copy.shape, BF16), pltpu.SemaphoreType.DMA],
        input_output_aliases={3: 0},
        cost_estimate=cost(1 << 16),
        compiler_params=PARAMS,
    )(place.reshape(1), shard, copy, before)


def on_device(inner_weights, outer_weights, outer_momentum):
    shard = inner_weights[0]
    rows_here, columns = shard.shape
    replicas = lax.axis_size("rep")
    blocks = lax.axis_size("fsdp")
    quarter = rows_here // replicas
    group = quarter // blocks
    rep = lax.axis_index("rep")
    chip, core = rep // 2, rep % 2
    outer_here = outer_weights[:, 0]
    momentum_here = outer_momentum[:, 0]
    ring = blocks // 2
    order = [half + (FIRST + z) % ring for half in (0, ring) for z in range(ring)]

    def exchange(value):
        return lax.all_to_all(
            value, "fsdp", split_axis=0, concat_axis=0, axis_index_groups=[order], tiled=True
        )

    def turn(value, by):
        halves = value.reshape(2, ring, *value.shape[1:])
        halves = jnp.concatenate([halves[:, by:], halves[:, :by]], axis=1)
        return halves.reshape(value.shape)

    def swap(value, i):
        return lax.ppermute(value, "rep", [(r, r ^ i) for r in range(replicas)])

    parts = shard.reshape(2, 2 * quarter, columns)
    state_part, other = state_and_other(chip, outer_here, momentum_here, parts)
    state_rows = turn(exchange(state_part), ring - FIRST).reshape(quarter, columns)

    mine = lax.dynamic_index_in_dim(parts, chip, 0, keepdims=False)
    pair = (mine.astype(F32) + swap(other, 2).astype(F32)).reshape(2, quarter, columns)
    pair_mine = lax.dynamic_index_in_dim(pair, core, 0, keepdims=False)
    pair_other = lax.dynamic_index_in_dim(pair, 1 - core, 0, keepdims=False)
    total = pair_mine + swap(pair_other.astype(BF16), 1).astype(F32)

    sent = turn(total.astype(BF16).reshape(blocks, group, columns), FIRST)
    sent, total = lax.optimization_barrier((sent, total))
    inner_total = exchange(sent)

    copy = (state_rows.astype(F32) + 0.3325 * total).astype(BF16)
    beside = swap(copy, 1)
    across = swap(copy, 2)
    diagonal = swap(across, 1)
    mixed, rest = mix(rep, shard, [copy, beside, across])
    mixed = mix_rest(rep ^ 3, rest, diagonal, mixed)

    new_outer, new_momentum = update(inner_total, outer_here, momentum_here)
    return (mixed[None], new_outer[:, None], new_momentum[:, None])


def solution(mesh):
    in_specs = (
        P("rep", "fsdp", "tp"),
        P(None, ("rep", "fsdp"), None, "tp"),
        P(None, ("rep", "fsdp"), None, "tp"),
    )
    out_specs = (
        P("rep", "fsdp", "tp"),
        P(None, ("rep", "fsdp"), None, "tp"),
        P(None, ("rep", "fsdp"), None, "tp"),
    )
    return jax.shard_map(
        on_device, mesh=mesh, in_specs=in_specs, out_specs=out_specs, check_vma=False
    )
```
